256 devices in a mesh: row: 32 (over y_hi, z, core), col: 8 (over x, y_lo).
Axes of the slice: x: 4, y: 4 (y_hi: 2, y_lo: 2; y = y_hi * 2 + y_lo), z: 8, core: 2. Of those that a mesh axis runs over, the one named last changes fastest.
Arguments:
- blocks: bfloat16 [320, 288, 128, 128], P('row', 'col')
- slot_cols: int32 [320, 288], P('row', 'col'), may hold values from 0 to 39, as said below
- counts: int32 [320, 8], P('row', 'col'), may hold values from 2 to 36, as said below
- demand: bfloat16 [40960, 128], P('col'), may hold values from 0.1 to 10
- value_added: float32 [40960], P('col'), may hold values from 0.5 to 5
Outputs:
- propagated: bfloat16 [40960, 128], P('row')
The draws below stay inside these ranges and needn't reach their ends.
Inputs may be any that keep to these rules, and one draw needn't show every extreme that they name: `counts`: some block row has all 36 slots live in every column group; live slots come first in each group. `slot_cols`: within one block row and column group the 36 slots name distinct column blocks.
All inputs are finite; a program needn't handle non-finite values.
Results may differ from the reference program's by a relative error of at most 0.0042.
Values may be sent and summed in bfloat16 or wider, within the bound.
A program may use at most 128 MiB of HBM per device.

```python
import math
import jax
import jax.numpy as jnp
from jax import lax

BS = 128
DC = 128
P_SIZE = 36
NB = 320
CB = 40
N_COL = 8


def pattern(key):
    base = jax.random.fold_in(key, 7)
    key_heavy, key_chosen, key_light, key_order = jax.random.split(base, 4)
    heavy = jax.random.randint(key_heavy, (NB, 1), 0, 6) == 0
    chosen = jax.random.randint(key_chosen, (), 0, NB)
    heavy = heavy | (jnp.arange(NB)[:, None] == chosen)
    light = jax.random.randint(key_light, (NB, N_COL), 2, max(P_SIZE // 3, 2) + 1)
    counts = jnp.where(heavy, P_SIZE, light).astype(jnp.int32)
    scores = jax.random.randint(key_order, (NB, N_COL, CB), 0, 1 << 20) * CB + jnp.arange(CB)[None, None, :]
    order = jnp.argsort(scores, axis=-1, stable=True)[:, :, :P_SIZE]
    return (counts, order.reshape(NB, N_COL * P_SIZE).astype(jnp.int32))


def draw_counts(key, part):
    return pattern(key)[0]


def draw_slot_cols(key, part):
    return pattern(key)[1]


def draw_blocks(key, part):
    base = jax.random.fold_in(key, 11)
    key_entry, key_block, key_column = jax.random.split(base, 3)
    slots = N_COL * P_SIZE
    block_scale = jnp.exp(jax.random.uniform(key_block, (NB, slots, 1, 1), minval=math.log(0.03), maxval=math.log(30.0)))
    column_scale = jnp.exp(jax.random.uniform(key_column, (NB, slots, 1, BS), minval=0.0, maxval=math.log(10.0)))
    factor = 1.0 / (BS * N_COL * P_SIZE)
    uniform_part = jax.random.uniform(key_entry, (NB, slots, BS, BS), minval=0.0, maxval=1.0)
    spread_ratio = 2000.0
    entries = 0.5 / math.log(1.0 + spread_ratio) / (uniform_part + 1.0 / spread_ratio)
    values = entries * block_scale * column_scale * factor
    return values.astype(jnp.bfloat16)


def draw_demand(key, part):
    base = jax.random.fold_in(key, 13)
    key_own, key_shared = jax.random.split(base, 2)
    groups = NB * BS // 16
    own_reach = 1.15
    shared_reach = 1.15
    own_part = jax.random.uniform(key_own, (groups, 16, DC), minval=-own_reach, maxval=own_reach)
    shared_part = jax.random.uniform(key_shared, (groups, 1, DC), minval=-shared_reach, maxval=shared_reach)
    values = jnp.exp(own_part + shared_part).reshape(NB * BS, DC)
    return values.astype(jnp.bfloat16)


def block_levels(stream_key, dims, cuts, smallest, high):
    def one(dim, shards_of):
        steps = jax.random.uniform(jax.random.fold_in(jax.random.fold_in(stream_key, 6), dim), (shards_of,), jnp.float32, smallest / len(cuts), high / len(cuts))
        return jnp.repeat(jnp.exp(steps), dims[dim] // shards_of).reshape((-1,) + (1,) * (len(dims) - dim - 1))

    level = one(*cuts[0])
    for cut in cuts[1:]:
        level = level * one(*cut)
    return level


def setup_inputs(seed: int = 0) -> dict:
    splits = jax.random.split(jax.random.key(seed), 6)
    return {
        "blocks": draw_blocks(jax.random.fold_in(splits[5], 71), 0),
        "slot_cols": draw_slot_cols(jax.random.fold_in(splits[5], 71), 0),
        "counts": draw_counts(jax.random.fold_in(splits[5], 71), 0),
        "demand": draw_demand(jax.random.fold_in(splits[5], 71), 0),
        "value_added": jnp.clip(jnp.exp(math.log(5.0) - 2.3025851 * jax.random.uniform(splits[4], (NB * BS,), jnp.float32) ** block_levels(splits[4], (NB * BS,), ((0, 8),), -0.2, 0.2)), 0.5, 5.0),
    }


def reference(blocks, slot_cols, counts, demand, value_added):
    slots = blocks.shape[1]
    position = jnp.arange(slots, dtype=jnp.int32)
    group_of = position // P_SIZE
    columns = (group_of[None, :] * CB + slot_cols).astype(jnp.int32)
    live_slots = ((position % P_SIZE)[None, :] < counts[:, group_of]).astype(jnp.float32)
    column_sums = lax.map(lambda zblock: jnp.sum(zblock.astype(jnp.float32), axis=1), blocks)
    column_sums = column_sums * live_slots[:, :, None]
    totals = jax.ops.segment_sum(column_sums.reshape(-1, BS), columns.reshape(-1), num_segments=NB)
    totals = totals.reshape(-1) + value_added
    inverse = (1.0 / totals).reshape(NB, BS)

    def layer(source):
        def one_row(items):
            zblock, column_row, live_row = items
            scaling = inverse[column_row] * live_row[:, None]
            coefficients = (zblock.astype(jnp.float32) * scaling[:, None, :]).astype(jnp.bfloat16)
            picked = source[column_row]
            return jnp.einsum("sij,sjk->ik", coefficients.astype(jnp.float32), picked.astype(jnp.float32))
        return lax.map(one_row, (blocks, columns, live_slots))

    layer_one = layer(demand.reshape(NB, BS, DC)).astype(jnp.bfloat16)
    layer_two = layer(layer_one)
    result = (layer_one.astype(jnp.float32) + layer_two).astype(jnp.bfloat16)
    return result.reshape(NB * BS, DC)
```

```python
import functools

import jax
import jax.numpy as jnp
from jax import lax
from jax.experimental import pallas as pl
from jax.experimental.pallas import tpu as pltpu
from jax.sharding import PartitionSpec as P

MESH = pl.DeviceIdType.MESH
HIGH = 2
CORES = 2


def kernel(
    rows, n,
    blocks, cols_s, cols_v, counts_s, demand, added, out,
    zbuf, sums, tsend, trecv, qsend, qrecv, tall, spread, scaled,
    part, rs_recv, part2, rs_recv2, zg, source, piece,
    zsem, t_send, t_recv, q_send, q_recv, a_send, a_recv,
    rs_send, rs_sem, rs_send2, rs_sem2, g_send, g_recv, p_send, p_recv,
    c_send, c_recv, o_send, o_recv, o_local,
):
    zs = rows // (HIGH * CORES)
    rb, slots, bs = zbuf.shape[0], zbuf.shape[1], zbuf.shape[2]
    cb = demand.shape[0]
    per_z = cb // zs
    targets = n // HIGH
    span = zs // targets
    tile = bs // n
    batches = rs_sem.shape[0]
    step = rb // batches
    row, col = lax.axis_index("row"), lax.axis_index("col")
    core = row % CORES
    z = (row // CORES) % zs
    high = row // (CORES * zs)

    def rid(h, zz, k):
        return (h * zs + zz) * CORES + k

    def remote(src, dst, send, recv, to):
        return pltpu.make_async_remote_copy(
            src_ref=src, dst_ref=dst, send_sem=send, recv_sem=recv, device_id=to, device_id_type=MESH
        )

    def each(count, fn, first=0):
        def body(i, c):
            fn(i)
            return c

        lax.fori_loop(first, count, body, 0)

    def load(b):
        return pltpu.make_async_copy(blocks.at[b], zbuf.at[b], zsem.at[b])

    each(rb, lambda b: load(b).start())

    barrier = pltpu.get_barrier_semaphore()

    def greet(to):
        pl.semaphore_signal(barrier, inc=1, device_id=to, device_id_type=MESH)

    each(zs, lambda d: greet((rid(high, (z + d) % zs, core), col)), 1)
    greet((rid(high, z, 1 - core), col))
    greet((rid(1 - high, z, 1 - core), col))
    each(n, lambda d: greet((row, (col + d) % n)), 1)
    each(n, lambda d: greet((rid(1 - high, z, core), d)))

    group = lax.broadcasted_iota(jnp.int32, (cb, slots), 0)
    slot = lax.broadcasted_iota(jnp.int32, (cb, slots), 1)

    def add_row(b, total):
        load(b).wait()
        for s in range(slots):
            sums[pl.ds(s, 1), :] = jnp.sum(zbuf[b, s].astype(jnp.float32), axis=0, keepdims=True)
        hit = (group == cols_v[pl.ds(b, 1), :]) & (slot < counts_s[b, 0])
        return total + jnp.dot(
            hit.astype(jnp.float32), sums[...], precision=lax.Precision.HIGHEST,
            preferred_element_type=jnp.float32,
        )

    total = lax.fori_loop(0, rb, add_row, jnp.zeros((cb, bs), jnp.float32))
    for k in range(zs):
        tsend[k] = total[k * per_z : (k + 1) * per_z]

    pl.semaphore_wait(barrier, (zs - 1) + 2 + (n - 1) + n)

    def t_copy(d):
        to = (z + d) % zs
        return remote(
            tsend.at[to], trecv.at[d - 1], t_send.at[d - 1], t_recv.at[d - 1], (rid(high, to, core), col)
        )

    each(zs, lambda d: t_copy(d).start(), 1)
    each(zs, lambda d: t_copy(d).wait(), 1)
    mine = tsend[z]
    for d in range(zs - 1):
        mine = mine + trecv[d]
    qsend[...] = mine
    quad = [
        remote(qsend, qrecv.at[i], q_send.at[i], q_recv.at[i], (rid(h, z, k), col))
        for i, (h, k) in enumerate(((high, 1 - core), (1 - high, core), (1 - high, 1 - core)))
    ]
    for copy in quad:
        copy.start()
    for copy in quad:
        copy.wait()
    tall[z] = (mine + qrecv[0]) + (qrecv[1] + qrecv[2])

    def a_copy(d):
        return remote(
            tall.at[z], tall.at[z], a_send.at[d - 1], a_recv.at[d - 1], (rid(high, (z + d) % zs, core), col)
        )

    def a_arrived(d):
        at = tall.at[(z + zs - d) % zs]
        remote(at, at, a_send.at[d - 1], a_recv.at[d - 1], (row, col)).wait_recv()

    each(zs, lambda d: a_copy(d).start(), 1)
    each(zs, a_arrived, 1)
    each(zs, lambda d: a_copy(d).wait_send(), 1)

    totals = jnp.concatenate([tall[k] for k in range(zs)], axis=0) + added[...]
    inverse = 1.0 / totals
    padded = jnp.concatenate([inverse, jnp.zeros((bs - cb, bs), jnp.float32)], axis=0)
    turned = padded.T
    for j in range(cb):
        wide = jnp.broadcast_to(turned[:, j : j + 1], (bs, bs))
        spread[j] = wide
        scaled[j] = (demand[j].astype(jnp.float32) * wide).astype(jnp.bfloat16)
    scaled[cb] = jnp.zeros((bs, bs), jnp.bfloat16)

    def layer(into, recv, send_sem, recv_sem):
        def rs_copy(batch, d):
            to = (col + d) % n
            at = pl.ds(batch * step, step)
            return remote(
                into.at[at, to], recv.at[d - 1, at], send_sem.at[batch, d - 1], recv_sem.at[batch, d - 1],
                (row, to),
            )

        def one(b):
            live = counts_s[b, 0]
            acc = jnp.zeros((bs, bs), jnp.float32)
            for s in range(0, slots, 2):
                at = [jnp.where(t < live, cols_s[b, t], cb) for t in (s, s + 1)]
                left = jnp.concatenate([zbuf[b, s], zbuf[b, s + 1]], axis=1)
                right = jnp.concatenate([scaled[at[0]], scaled[at[1]]], axis=0)
                acc = acc + jnp.dot(left, right, preferred_element_type=jnp.float32)
            into[b] = acc.astype(jnp.bfloat16).reshape(n, tile, bs)

        for batch in range(batches):
            each((batch + 1) * step, one, batch * step)
            each(n, lambda d, batch=batch: rs_copy(batch, d).start(), 1)
        for batch in range(batches):
            each(n, lambda d, batch=batch: rs_copy(batch, d).wait(), 1)

    def summed(b, own, recv):
        acc = own[b, col].astype(jnp.float32)
        for d in range(n - 1):
            acc = acc + recv[d, b].astype(jnp.float32)
        return acc

    layer(part, rs_recv, rs_send, rs_sem)
    for b in range(rb):
        zg[z, b] = summed(b, part, rs_recv).astype(jnp.bfloat16)

    def g_copy(d):
        return remote(
            zg.at[z], zg.at[z], g_send.at[d - 1], g_recv.at[d - 1], (rid(high, (z + d) % zs, core), col)
        )

    def g_arrived(d):
        at = zg.at[(z + zs - d) % zs]
        remote(at, at, g_send.at[d - 1], g_recv.at[d - 1], (row, col)).wait_recv()

    each(zs, lambda d: g_copy(d).start(), 1)
    each(zs, g_arrived, 1)
    each(zs, lambda d: g_copy(d).wait_send(), 1)

    def p_parts(i):
        h, k = i // targets, i % targets
        to = high * targets + k
        here = (h == high) & (to == col)
        src = zg.at[pl.ds(k * span, span)]
        dst = source.at[:, core, :, col]
        far = remote(src, dst, p_send.at[i], p_recv.at[col], (rid(h, z, core), to))
        near = pltpu.make_async_copy(src, dst, p_recv.at[col])
        return here, far, near

    def p_start(i):
        here, far, near = p_parts(i)

        @pl.when(here)
        def _():
            near.start()

        @pl.when(jnp.logical_not(here))
        def _():
            far.start()

    each(n, p_start)

    def c_copy(c):
        at = source.at[:, core, :, c]
        return remote(at, at, c_send.at[c], c_recv.at[c], (rid(high, z, 1 - core), col))

    def forward(c):
        at = source.at[:, core, :, c]
        pltpu.make_async_copy(at, at, p_recv.at[c]).wait()
        c_copy(c).start()

    each(n, forward)

    def c_arrived(c):
        at = source.at[:, 1 - core, :, c]
        remote(at, at, c_send.at[c], c_recv.at[c], (row, col)).wait_recv()

    each(n, c_arrived)

    def p_sent(i):
        here, far, near = p_parts(i)

        @pl.when(jnp.logical_not(here))
        def _():
            far.wait_send()

    each(n, p_sent)
    each(n, lambda c: c_copy(c).wait_send())

    def scale(j):
        q, b = j // rb, j % rb
        value = source[q // CORES, q % CORES, b].reshape(bs, bs).astype(jnp.float32)
        scaled[j] = (value * spread[j]).astype(jnp.bfloat16)

    each(cb, scale)

    layer(part2, rs_recv2, rs_send2, rs_sem2)
    for b in range(rb):
        piece[b] = (zg[z, b].astype(jnp.float32) + summed(b, part2, rs_recv2)).astype(jnp.bfloat16)

    def o_copy(d):
        return remote(
            piece, out.at[:, col], o_send.at[d - 1], o_recv.at[d - 1], (row, (col + d) % n)
        )

    def o_arrived(d):
        at = out.at[:, (col + n - d) % n]
        remote(piece, at, o_send.at[d - 1], o_recv.at[d - 1], (row, col)).wait_recv()

    each(n, lambda d: o_copy(d).start(), 1)
    own = pltpu.make_async_copy(piece, out.at[:, col], o_local)
    own.start()
    each(n, o_arrived, 1)
    each(n, lambda d: o_copy(d).wait_send(), 1)
    own.wait()


def body(rows, n, blocks, slot_cols, counts, demand, value_added):
    rb, slots, bs = blocks.shape[0], blocks.shape[1], blocks.shape[2]
    cb = demand.shape[0] // bs
    zs = rows // (HIGH * CORES)
    span = zs // (n // HIGH)
    tile = bs // n
    batches = 2
    bf, f32, dma = jnp.bfloat16, jnp.float32, pltpu.SemaphoreType.DMA
    vmem, smem, hbm = (
        pl.BlockSpec(memory_space=pltpu.VMEM), pl.BlockSpec(memory_space=pltpu.SMEM), pl.BlockSpec(memory_space=pl.ANY)
    )
    result = pl.pallas_call(
        functools.partial(kernel, rows, n),
        out_shape=jax.ShapeDtypeStruct((rb, n, tile, bs), bf),
        in_specs=[hbm, smem, vmem, smem, vmem, vmem],
        out_specs=hbm,
        scratch_shapes=[
            pltpu.VMEM((rb, slots, bs, bs), bf),
            pltpu.VMEM((slots, bs), f32),
            pltpu.VMEM((zs, cb // zs, bs), f32),
            pltpu.VMEM((zs - 1, cb // zs, bs), f32),
            pltpu.VMEM((cb // zs, bs), f32),
            pltpu.VMEM((3, cb // zs, bs), f32),
            pltpu.VMEM((zs, cb // zs, bs), f32),
            pltpu.VMEM((cb, bs, bs), f32),
            pltpu.VMEM((cb + 1, bs, bs), bf),
            pltpu.VMEM((rb, n, tile, bs), bf),
            pltpu.VMEM((n - 1, rb, tile, bs), bf),
            pltpu.VMEM((rb, n, tile, bs), bf),
            pltpu.VMEM((n - 1, rb, tile, bs), bf),
            pltpu.VMEM((zs, rb, tile, bs), bf),
            pltpu.VMEM((span, CORES, rb, n, tile, bs), bf),
            pltpu.VMEM((rb, tile, bs), bf),
            dma((rb,)),
            dma((zs - 1,)), dma((zs - 1,)),
            dma((3,)), dma((3,)),
            dma((zs - 1,)), dma((zs - 1,)),
            dma((batches, n - 1)), dma((batches, n - 1)),
            dma((batches, n - 1)), dma((batches, n - 1)),
            dma((zs - 1,)), dma((zs - 1,)),
            dma((n,)), dma((n,)),
            dma((n,)), dma((n,)),
            dma((n - 1,)), dma((n - 1,)),
            dma(()),
        ],
        compiler_params=pltpu.CompilerParams(
            collective_id=0, has_side_effects=True, vmem_limit_bytes=56 * 2**20
        ),
    )(
        blocks, slot_cols, slot_cols, counts, demand.reshape(cb, bs, bs), value_added.reshape(cb, bs)
    )
    return result.reshape(rb * bs, bs)


def solution(mesh):
    rows, n = mesh.shape["row"], mesh.shape["col"]
    return jax.shard_map(
        functools.partial(body, rows, n),
        mesh=mesh,
        in_specs=(
            P("row", "col", None, None),
            P("row", "col"),
            P("row", "col"),
            P("col", None),
            P("col"),
        ),
        out_specs=P("row", None),
        check_vma=False,
    )
```

```python
import functools

import jax
import jax.numpy as jnp
from jax import lax
from jax.experimental import pallas as pl
from jax.experimental.pallas import tpu as pltpu
from jax.sharding import PartitionSpec as P

MESH = pl.DeviceIdType.MESH
HIGH = 2
CORES = 2
WIDE = 4


def kernel(
    rows, n,
    blocks, cols_s, cols_v, counts_s, demand_hbm, added, out,
    zbuf, demand, sums, tsend, trecv, bsend, brecv, tall, spread, scaled,
    part, rs_recv, part2, rs_recv2, first, source, piece,
    zsem, dsem, t_send, t_recv, b_send, b_recv, a_send, a_recv,
    rs_send, rs_sem, rs_send2, rs_sem2, p_send, p_recv,
    y_send, y_recv, c_send, c_recv, o_send, o_recv, o_local,
):
    zs = rows // (HIGH * CORES)
    rb, slots, bs = zbuf.shape[0], zbuf.shape[1], zbuf.shape[2]
    cb = demand.shape[0]
    per_core = cb // CORES
    chips = rows // CORES
    targets = n // HIGH
    tile = bs // n
    batches = rs_sem.shape[0]
    step = rb // batches
    lag = min(2, batches - 1)
    row, col = lax.axis_index("row"), lax.axis_index("col")
    core = row % CORES
    z = (row // CORES) % zs
    high = row // (CORES * zs)

    def rid(h, zz, k):
        return (h * zs + zz) * CORES + k

    def remote(src, dst, send, recv, to):
        return pltpu.make_async_remote_copy(
            src_ref=src, dst_ref=dst, send_sem=send, recv_sem=recv, device_id=to, device_id_type=MESH
        )

    def each(count, fn, first=0):
        def body(i, c):
            fn(i)
            return c

        lax.fori_loop(first, count, body, 0)

    def load(b):
        return pltpu.make_async_copy(blocks.at[b], zbuf.at[b], zsem.at[b])

    each(rb, lambda b: load(b).start())
    load_demand = pltpu.make_async_copy(demand_hbm, demand, dsem)
    load_demand.start()

    buyer = row // (rows // n)
    side = z % HIGH
    giver = rid(col // targets, (col % targets) * HIGH + high, core)
    is_self = (side == high) & (buyer == col)
    here = row // CORES

    def chip(d):
        return ((here + d) % chips) * CORES + core

    barrier = pltpu.get_barrier_semaphore()

    def greet(to):
        pl.semaphore_signal(barrier, inc=1, device_id=to, device_id_type=MESH)

    each(chips, lambda d: greet((chip(d), col)), 1)
    greet((rid(high, z, 1 - core), col))
    each(n, lambda d: greet((row, (col + d) % n)), 1)

    def greet_giver(c):
        @pl.when(jnp.logical_not((giver == row) & (c == col)))
        def _():
            greet((giver, c))

    each(n, greet_giver)

    group = lax.broadcasted_iota(jnp.int32, (cb, slots), 0)
    slot = lax.broadcasted_iota(jnp.int32, (cb, slots), 1)

    def add_row(b, total):
        load(b).wait()
        for s in range(slots):
            sums[pl.ds(s, 1), :] = jnp.sum(zbuf[b, s].astype(jnp.float32), axis=0, keepdims=True)
        hit = (group == cols_v[pl.ds(b, 1), :]) & (slot < counts_s[0, b])
        return total + jnp.dot(
            hit.astype(jnp.float32), sums[...], precision=lax.Precision.HIGHEST,
            preferred_element_type=jnp.float32,
        )

    total = lax.fori_loop(0, rb, add_row, jnp.zeros((cb, bs), jnp.float32))
    for k in range(CORES):
        tsend[k] = total[k * per_core : (k + 1) * per_core]
    load_demand.wait()

    pl.semaphore_wait(barrier, (chips - 1) + 1 + (n - 1) + zs - jnp.where(is_self, 1, 0))

    twin = (rid(high, z, 1 - core), col)
    swap = remote(tsend.at[1 - core], trecv, t_send, t_recv, twin)
    swap.start()
    swap.wait()
    mine = tsend[core] + trecv[...]
    bsend[...] = jnp.concatenate(
        [mine, jnp.zeros((bsend.shape[0] - per_core, bs), jnp.float32)], axis=0
    ).astype(jnp.bfloat16)

    def b_copy(d):
        return remote(bsend, brecv.at[d - 1], b_send.at[d - 1], b_recv.at[d - 1], (chip(d), col))

    each(chips, lambda d: b_copy(d).start(), 1)
    each(chips, lambda d: b_copy(d).wait_recv(), 1)
    for d in range(chips - 1):
        mine = mine + brecv[d].astype(jnp.float32)[:per_core]
    tall[core] = mine
    give_half = remote(tall.at[core], tall.at[core], a_send, a_recv, twin)
    give_half.start()
    each(chips, lambda d: b_copy(d).wait_send(), 1)
    give_half.wait_send()
    remote(tall.at[1 - core], tall.at[1 - core], a_send, a_recv, twin).wait_recv()

    totals = jnp.concatenate([tall[k] for k in range(CORES)], axis=0) + added[...]
    inverse = 1.0 / totals
    padded = jnp.concatenate([inverse, jnp.zeros((bs - cb, bs), jnp.float32)], axis=0)
    turned = padded.T
    for j in range(cb):
        wide = jnp.broadcast_to(turned[:, j : j + 1], (bs, bs))
        spread[j] = wide
        scaled[j] = (demand[j].astype(jnp.float32) * wide).astype(jnp.bfloat16)
    scaled[cb] = jnp.zeros((bs, bs), jnp.bfloat16)

    def layer(into, recv, send_sem, recv_sem, finish, after):
        def rs_copy(i, d):
            to = (col + d) % n
            at = pl.ds(i * step, step)
            return remote(
                into.at[to, at], recv.at[d - 1, at], send_sem.at[i, d - 1], recv_sem.at[i, d - 1], (row, to)
            )

        def compute(i):
            accs = [jnp.zeros((bs, bs), jnp.float32) for _ in range(step)]
            wide = WIDE if slots % WIDE == 0 else 2
            for s in range(0, slots, wide):
                for k in range(step):
                    b = i * step + k
                    live = counts_s[0, b]
                    at = [jnp.where(t < live, cols_s[b, t], cb) for t in range(s, s + wide)]
                    left = jnp.concatenate([zbuf[b, t] for t in range(s, s + wide)], axis=1)
                    right = jnp.concatenate([scaled[a] for a in at], axis=0)
                    accs[k] = accs[k] + jnp.dot(left, right, preferred_element_type=jnp.float32)
            for k in range(step):
                into[:, i * step + k] = accs[k].astype(jnp.bfloat16).reshape(n, tile, bs)

        def reduce(i):
            each(n, lambda d: rs_copy(i, d).wait_recv(), 1)
            for k in range(step):
                b = i * step + k
                acc = into[col, b].astype(jnp.float32)
                for d in range(n - 1):
                    acc = acc + recv[d, b].astype(jnp.float32)
                finish(b, acc)
            after(i)

        def batch(i):
            compute(i)
            each(n, lambda d: rs_copy(i, d).start(), 1)

            @pl.when(i >= lag)
            def _():
                reduce(i - lag)

        each(batches, batch)
        each(batches, reduce, batches - lag)
        return lambda: each(batches, lambda i: each(n, lambda d: rs_copy(i, d).wait_send(), 1))

    def keep(b, acc):
        first[b] = acc.astype(jnp.bfloat16)

    def p_copy(i, d):
        src = first.at[pl.ds(i * step, step)]
        dst = source.at[side, core, i, col]
        to = (rid(side, (z + d) % zs, core), buyer)
        return src, dst, remote(src, dst, p_send.at[i, d], p_recv.at[i, col], to)

    def spread_out(i):
        src, dst, far = p_copy(i, 0)

        @pl.when(is_self)
        def _():
            pltpu.make_async_copy(src, dst, p_recv.at[i, col]).start()

        @pl.when(jnp.logical_not(is_self))
        def _():
            far.start()

        each(zs, lambda d: p_copy(i, d)[2].start(), 1)

    def spread_sent(i):
        @pl.when(jnp.logical_not(is_self))
        def _():
            p_copy(i, 0)[2].wait_send()

        each(zs, lambda d: p_copy(i, d)[2].wait_send(), 1)

    sent_one = layer(part, rs_recv, rs_send, rs_sem, keep, spread_out)

    def y_copy(i):
        at = source.at[high, core, i]
        return remote(at, at, y_send.at[i], y_recv.at[i], (rid(1 - high, z, core), col))

    def y_arrived(i):
        at = source.at[1 - high, core, i]
        remote(at, at, y_send.at[i], y_recv.at[i], (row, col)).wait_recv()

    def c_copy(i, h):
        at = source.at[h, core, i]
        return remote(at, at, c_send.at[i, h], c_recv.at[i, h], twin)

    def c_arrived(i, h):
        at = source.at[h, 1 - core, i]
        remote(at, at, c_send.at[i, h], c_recv.at[i, h], twin).wait_recv()

    def pass_on(i):
        def p_arrived(c):
            at = source.at[high, core, i, c]
            pltpu.make_async_copy(at, at, p_recv.at[i, c]).wait()

        each(n, p_arrived)
        y_copy(i).start()
        c_copy(i, high).start()

    def pass_back(i):
        y_arrived(i)
        c_copy(i, 1 - high).start()

    def both(i):
        pass_on(i)

        @pl.when(i >= 1)
        def _():
            pass_back(i - 1)

    each(batches, both)
    pass_back(batches - 1)

    def arrived(i):
        for h in range(HIGH):
            c_arrived(i, h)

    each(batches, arrived)

    def scale(j):
        q, b = j // rb, j % rb
        value = source[q // CORES, q % CORES, b // step, :, b % step]
        value = value.reshape(bs, bs).astype(jnp.float32)
        scaled[j] = (value * spread[j]).astype(jnp.bfloat16)

    each(cb, scale)

    def result(b, acc):
        piece[b] = (first[b].astype(jnp.float32) + acc).astype(jnp.bfloat16)

    def o_copy(i, d):
        at = pl.ds(i * step, step)
        return remote(
            piece.at[at], out.at[at, col], o_send.at[i, d - 1], o_recv.at[i, d - 1], (row, (col + d) % n)
        )

    def o_own(i):
        at = pl.ds(i * step, step)
        return pltpu.make_async_copy(piece.at[at], out.at[at, col], o_local.at[i])

    def give(i):
        each(n, lambda d: o_copy(i, d).start(), 1)
        o_own(i).start()

    def o_arrived(i, d):
        at = pl.ds(i * step, step)
        remote(
            piece.at[at], out.at[at, (col + n - d) % n], o_send.at[i, d - 1], o_recv.at[i, d - 1], (row, col)
        ).wait_recv()

    sent_two = layer(part2, rs_recv2, rs_send2, rs_sem2, result, give)
    each(batches, spread_sent)

    def passed(i):
        y_copy(i).wait_send()
        for h in range(HIGH):
            c_copy(i, h).wait_send()

    each(batches, passed)
    sent_one()
    sent_two()
    each(batches, lambda i: each(n, lambda d: o_arrived(i, d), 1))
    each(batches, lambda i: each(n, lambda d: o_copy(i, d).wait_send(), 1))
    each(batches, lambda i: o_own(i).wait())


def body(rows, n, blocks, slot_cols, counts, demand, value_added):
    rb, slots, bs = blocks.shape[0], blocks.shape[1], blocks.shape[2]
    cb = demand.shape[0] // bs
    zs = rows // (HIGH * CORES)
    tile = bs // n
    step = 2
    batches = rb // step
    per_core, chips = cb // CORES, rows // CORES
    bf, f32, dma = jnp.bfloat16, jnp.float32, pltpu.SemaphoreType.DMA
    vmem, smem, hbm = (
        pl.BlockSpec(memory_space=pltpu.VMEM), pl.BlockSpec(memory_space=pltpu.SMEM), pl.BlockSpec(memory_space=pl.ANY)
    )
    result = pl.pallas_call(
        functools.partial(kernel, rows, n),
        out_shape=jax.ShapeDtypeStruct((rb, n, tile, bs), bf),
        in_specs=[hbm, smem, vmem, smem, hbm, vmem],
        out_specs=hbm,
        scratch_shapes=[
            pltpu.VMEM((rb, slots, bs, bs), bf),
            pltpu.VMEM((cb, bs, bs), bf),
            pltpu.VMEM((slots, bs), f32),
            pltpu.VMEM((CORES, per_core, bs), f32),
            pltpu.VMEM((per_core, bs), f32),
            pltpu.VMEM((-(-per_core // 16) * 16, bs), bf),
            pltpu.VMEM((chips - 1, -(-per_core // 16) * 16, bs), bf),
            pltpu.VMEM((CORES, per_core, bs), f32),
            pltpu.VMEM((cb, bs, bs), f32),
            pltpu.VMEM((cb + 1, bs, bs), bf),
            pltpu.VMEM((n, rb, tile, bs), bf),
            pltpu.VMEM((n - 1, rb, tile, bs), bf),
            pltpu.VMEM((n, rb, tile, bs), bf),
            pltpu.VMEM((n - 1, rb, tile, bs), bf),
            pltpu.VMEM((rb, tile, bs), bf),
            pltpu.VMEM((HIGH, CORES, batches, n, step, tile, bs), bf),
            pltpu.VMEM((rb, tile, bs), bf),
            dma((rb,)), dma(()),
            dma(()), dma(()),
            dma((chips - 1,)), dma((chips - 1,)),
            dma(()), dma(()),
            dma((batches, n - 1)), dma((batches, n - 1)),
            dma((batches, n - 1)), dma((batches, n - 1)),
            dma((batches, zs)), dma((batches, n)),
            dma((batches,)), dma((batches,)),
            dma((batches, HIGH)), dma((batches, HIGH)),
            dma((batches, n - 1)), dma((batches, n - 1)),
            dma((batches,)),
        ],
        compiler_params=pltpu.CompilerParams(
            collective_id=0, has_side_effects=True, vmem_limit_bytes=56 * 2**20
        ),
    )(
        blocks, slot_cols, slot_cols, counts.T, demand.reshape(cb, bs, bs), value_added.reshape(cb, bs)
    )
    return result.reshape(rb * bs, bs)


def solution(mesh):
    rows, n = mesh.shape["row"], mesh.shape["col"]
    return jax.shard_map(
        functools.partial(body, rows, n),
        mesh=mesh,
        in_specs=(
            P("row", "col", None, None),
            P("row", "col"),
            P("row", "col"),
            P("col", None),
            P("col"),
        ),
        out_specs=P("row", None),
        check_vma=False,
    )
```

```python
import functools

import jax
import jax.numpy as jnp
from jax import lax
from jax.experimental import pallas as pl
from jax.experimental.pallas import tpu as pltpu
from jax.sharding import PartitionSpec as P

MESH = pl.DeviceIdType.MESH
HIGH = 2
CORES = 2
WIDE = 4


def kernel(
    rows, n, groups,
    blocks, cols_s, cols_v, counts_s, demand_hbm, added, out,
    zbuf, demand, sums, tsend, trecv, bsend, brecv, tall, spread, scaled,
    part, rs_recv, part2, rs_recv2, first, source, piece, places, place_s, so_far,
    zsem, dsem, place_sem, t_send, t_recv, b_send, b_recv, a_send, a_recv,
    rs_send, rs_sem, rs_send2, rs_sem2, p_send, p_recv,
    y_send, y_recv, c_send, c_recv, o_send, o_recv, o_local,
):
    zs = rows // (HIGH * CORES)
    rb, slots, bs = zbuf.shape[0], zbuf.shape[1], zbuf.shape[2]
    cb = demand.shape[0]
    per_core = cb // CORES
    chips = rows // CORES
    targets = n // HIGH
    tile = bs // n
    batches = len(groups)
    step = 2
    row, col = lax.axis_index("row"), lax.axis_index("col")
    core = row % CORES
    z = (row // CORES) % zs
    high = row // (CORES * zs)

    def rid(h, zz, k):
        return (h * zs + zz) * CORES + k

    def remote(src, dst, send, recv, to):
        return pltpu.make_async_remote_copy(
            src_ref=src, dst_ref=dst, send_sem=send, recv_sem=recv, device_id=to, device_id_type=MESH
        )

    def span(g):
        return pl.ds(groups[g][0], groups[g][1] - groups[g][0])

    def each(count, fn, first=0):
        def body(i, c):
            fn(i)
            return c

        lax.fori_loop(first, count, body, 0)

    def settle(ref, sem):
        pltpu.make_async_copy(ref, ref, sem).wait()

    def load(b):
        return pltpu.make_async_copy(blocks.at[b], zbuf.at[b], zsem.at[b])

    each(rb, lambda b: load(b).start())
    load_demand = pltpu.make_async_copy(demand_hbm, demand, dsem)
    load_demand.start()

    buyer = row // (rows // n)
    side = z % HIGH
    giver = rid(col // targets, (col % targets) * HIGH + high, core)
    is_self = (side == high) & (buyer == col)
    here = row // CORES

    def chip(d):
        return ((here + d) % chips) * CORES + core

    barrier = pltpu.get_barrier_semaphore()

    def greet(to):
        pl.semaphore_signal(barrier, inc=1, device_id=to, device_id_type=MESH)

    each(chips, lambda d: greet((chip(d), col)), 1)
    greet((rid(high, z, 1 - core), col))
    each(n, lambda d: greet((row, (col + d) % n)), 1)

    def greet_giver(c):
        @pl.when(jnp.logical_not((giver == row) & (c == col)))
        def _():
            greet((giver, c))

    each(n, greet_giver)

    group = lax.broadcasted_iota(jnp.int32, (cb, slots), 0)
    slot = lax.broadcasted_iota(jnp.int32, (cb, slots), 1)

    lane = lax.broadcasted_iota(jnp.int32, (cb, bs), 1)

    def add_row(b, carry):
        total, place = carry
        load(b).wait()
        for s in range(slots):
            sums[pl.ds(s, 1), :] = jnp.sum(zbuf[b, s].astype(jnp.float32), axis=0, keepdims=True)
        hit = (group == cols_v[pl.ds(b, 1), :]) & (slot < counts_s[0, b])
        found = jnp.sum(jnp.where(hit, slot + 1, 0), axis=1, keepdims=True)
        place = jnp.where(lane == b, found, place)
        total = total + jnp.dot(
            hit.astype(jnp.float32), sums[...], precision=lax.Precision.HIGHEST,
            preferred_element_type=jnp.float32,
        )
        return total, place

    total, place = lax.fori_loop(
        0, rb, add_row, (jnp.zeros((cb, bs), jnp.float32), jnp.zeros((cb, bs), jnp.int32))
    )
    places[...] = place
    move = pltpu.make_async_copy(places, place_s, place_sem)
    move.start()
    for k in range(CORES):
        tsend[k] = total[k * per_core : (k + 1) * per_core]
    load_demand.wait()
    move.wait()

    pl.semaphore_wait(barrier, (chips - 1) + 1 + (n - 1) + zs - jnp.where(is_self, 1, 0))

    twin = (rid(high, z, 1 - core), col)
    swap = remote(tsend.at[1 - core], trecv, t_send, t_recv, twin)
    swap.start()
    swap.wait()
    mine = tsend[core] + trecv[...]
    bsend[...] = jnp.concatenate(
        [mine, jnp.zeros((bsend.shape[0] - per_core, bs), jnp.float32)], axis=0
    ).astype(jnp.bfloat16)

    def b_copy(d):
        return remote(bsend, brecv.at[d - 1], b_send, b_recv, (chip(d), col))

    each(chips, lambda d: b_copy(d).start(), 1)
    settle(brecv, b_recv)
    for d in range(chips - 1):
        mine = mine + brecv[d].astype(jnp.float32)[:per_core]
    tall[core] = mine
    give_half = remote(tall.at[core], tall.at[core], a_send, a_recv, twin)
    give_half.start()
    settle(brecv, b_send)
    give_half.wait_send()
    remote(tall.at[1 - core], tall.at[1 - core], a_send, a_recv, twin).wait_recv()

    totals = jnp.concatenate([tall[k] for k in range(CORES)], axis=0) + added[...]
    inverse = 1.0 / totals
    padded = jnp.concatenate([inverse, jnp.zeros((bs - cb, bs), jnp.float32)], axis=0)
    turned = padded.T
    for j in range(cb):
        wide = jnp.broadcast_to(turned[:, j : j + 1], (bs, bs))
        spread[j] = wide
        scaled[j] = (demand[j].astype(jnp.float32) * wide).astype(jnp.bfloat16)
    scaled[cb] = jnp.zeros((bs, bs), jnp.bfloat16)

    def exchange(into, recv, send_sem, recv_sem, finish, after):
        def rs_copy(g, d):
            to = (col + d) % n
            at = span(g)
            return remote(into.at[to, at], recv.at[d - 1, at], send_sem.at[g], recv_sem.at[g], (row, to))

        def start(g):
            each(n, lambda d: rs_copy(g, d).start(), 1)

        def reduce(g):
            settle(recv.at[:, span(g)], recv_sem.at[g])
            for b in range(*groups[g]):
                acc = into[col, b].astype(jnp.float32)
                for d in range(n - 1):
                    acc = acc + recv[d, b].astype(jnp.float32)
                finish(b, acc)
            after(g)

        def sent():
            for g in range(batches):
                settle(recv.at[:, span(g)], send_sem.at[g])

        return start, reduce, sent

    def product(acc, b, pairs):
        left = jnp.concatenate([zbuf[b, t] for t, _ in pairs], axis=1)
        right = jnp.concatenate([scaled[a] for _, a in pairs], axis=0)
        return acc + jnp.dot(left, right, preferred_element_type=jnp.float32)

    def compute(i):
        accs = [jnp.zeros((bs, bs), jnp.float32) for _ in range(step)]
        wide = WIDE if slots % WIDE == 0 else 2
        for s in range(0, slots, wide):
            for k in range(step):
                b = i * step + k
                live = counts_s[0, b]
                pairs = [(t, jnp.where(t < live, cols_s[b, t], cb)) for t in range(s, s + wide)]
                accs[k] = product(accs[k], b, pairs)
        for k in range(step):
            part[:, i * step + k] = accs[k].astype(jnp.bfloat16).reshape(n, tile, bs)

    def keep(b, acc):
        first[b] = acc.astype(jnp.bfloat16)

    def p_copy(i, d):
        src = first.at[span(i)]
        dst = source.at[side, core, span(i), col]
        to = (rid(side, (z + d) % zs, core), buyer)
        return src, dst, remote(src, dst, p_send.at[i, jnp.minimum(d, 1)], p_recv.at[i], to)

    def spread_out(i):
        src, dst, far = p_copy(i, 0)

        @pl.when(is_self)
        def _():
            pltpu.make_async_copy(src, dst, p_recv.at[i]).start()

        @pl.when(jnp.logical_not(is_self))
        def _():
            far.start()

        each(zs, lambda d: p_copy(i, d)[2].start(), 1)

    def spread_sent(i):
        @pl.when(jnp.logical_not(is_self))
        def _():
            p_copy(i, 0)[2].wait_send()

        settle(source.at[high, core, span(i), pl.ds(0, zs - 1)], p_send.at[i, 1])

    start_one, reduce_one, sent_one = exchange(part, rs_recv, rs_send, rs_sem, keep, spread_out)
    for g in range(batches):
        each(groups[g][1] // step, compute, groups[g][0] // step)
        start_one(g)
    for g in range(batches):
        reduce_one(g)

    def y_copy(i):
        at = source.at[high, core, span(i)]
        return remote(at, at, y_send.at[i], y_recv.at[i], (rid(1 - high, z, core), col))

    def y_arrived(i):
        at = source.at[1 - high, core, span(i)]
        remote(at, at, y_send.at[i], y_recv.at[i], (row, col)).wait_recv()

    def c_copy(i, h):
        at = source.at[h, core, span(i)]
        return remote(at, at, c_send.at[i, h], c_recv.at[i, h], twin)

    def c_arrived(i, h):
        at = source.at[h, 1 - core, span(i)]
        remote(at, at, c_send.at[i, h], c_recv.at[i, h], twin).wait_recv()

    def pass_on(i):
        settle(source.at[high, core, span(i)], p_recv.at[i])
        y_copy(i).start()
        c_copy(i, high).start()

    def pass_back(i):
        y_arrived(i)
        c_copy(i, 1 - high).start()

    def result(b, acc):
        piece[b] = (first[b].astype(jnp.float32) + acc).astype(jnp.bfloat16)

    def o_copy(i, d):
        at = span(i)
        return remote(
            piece.at[at], out.at[at, col], o_send.at[i], o_recv.at[i], (row, (col + d) % n)
        )

    def o_own(i):
        at = span(i)
        return pltpu.make_async_copy(piece.at[at], out.at[at, col], o_local.at[i])

    def give(i):
        each(n, lambda d: o_copy(i, d).start(), 1)
        o_own(i).start()

    start_two, reduce_two, sent_two = exchange(part2, rs_recv2, rs_send2, rs_sem2, result, give)

    def advance(g):
        lo, hi = groups[g]
        for h in range(HIGH):
            c_arrived(g, h)
        cols_of = [q * rb + b for q in range(HIGH * CORES) for b in range(lo, hi)]
        for j in cols_of:
            q, b = j // rb, j % rb
            value = source[q // CORES, q % CORES, b].reshape(bs, bs).astype(jnp.float32)
            scaled[j] = (value * spread[j]).astype(jnp.bfloat16)

        def rows_of(i):
            accs = [so_far[i * step + k] if g else jnp.zeros((bs, bs), jnp.float32) for k in range(step)]
            for s in range(0, len(cols_of), WIDE):
                for k in range(step):
                    b = i * step + k
                    pairs = []
                    for j in cols_of[s : s + WIDE]:
                        at = place_s[j, b]
                        pairs.append((jnp.maximum(at - 1, 0), jnp.where(at > 0, j, cb)))
                    accs[k] = product(accs[k], b, pairs)
            for k in range(step):
                if g < batches - 1:
                    so_far[i * step + k] = accs[k]
                else:
                    part2[:, i * step + k] = accs[k].astype(jnp.bfloat16).reshape(n, tile, bs)

        if g < batches - 1:
            each(rb // step, rows_of)
        else:
            for k in range(batches):
                each(groups[k][1] // step, rows_of, groups[k][0] // step)
                start_two(k)

    for g in range(batches):
        pass_on(g)
        if g >= 1:
            pass_back(g - 1)
        if g >= 2:
            advance(g - 2)
    pass_back(batches - 1)
    for g in range(max(batches - 2, 0), batches):
        advance(g)
    for g in range(batches):
        reduce_two(g)

    for g in range(batches):
        spread_sent(g)

    def passed(i):
        y_copy(i).wait_send()
        for h in range(HIGH):
            c_copy(i, h).wait_send()

    for g in range(batches):
        passed(g)
    sent_one()
    sent_two()

    for g in range(batches):
        like = rs_recv2.at[:, span(g)]
        settle(like, o_recv.at[g])
        settle(like, o_send.at[g])
        o_own(g).wait()


def body(rows, n, blocks, slot_cols, counts, demand, value_added):
    rb, slots, bs = blocks.shape[0], blocks.shape[1], blocks.shape[2]
    cb = demand.shape[0] // bs
    zs = rows // (HIGH * CORES)
    tile = bs // n
    cuts = sorted({0, rb * 2 // 5 // 2 * 2, rb * 4 // 5 // 2 * 2, rb})
    groups = tuple(zip(cuts, cuts[1:]))
    batches = len(groups)
    per_core, chips = cb // CORES, rows // CORES
    bf, f32, dma = jnp.bfloat16, jnp.float32, pltpu.SemaphoreType.DMA
    vmem, smem, hbm = (
        pl.BlockSpec(memory_space=pltpu.VMEM), pl.BlockSpec(memory_space=pltpu.SMEM), pl.BlockSpec(memory_space=pl.ANY)
    )
    result = pl.pallas_call(
        functools.partial(kernel, rows, n, groups),
        out_shape=jax.ShapeDtypeStruct((rb, n, tile, bs), bf),
        in_specs=[hbm, smem, vmem, smem, hbm, vmem],
        out_specs=hbm,
        scratch_shapes=[
            pltpu.VMEM((rb, slots, bs, bs), bf),
            pltpu.VMEM((cb, bs, bs), bf),
            pltpu.VMEM((slots, bs), f32),
            pltpu.VMEM((CORES, per_core, bs), f32),
            pltpu.VMEM((per_core, bs), f32),
            pltpu.VMEM((-(-per_core // 16) * 16, bs), bf),
            pltpu.VMEM((chips - 1, -(-per_core // 16) * 16, bs), bf),
            pltpu.VMEM((CORES, per_core, bs), f32),
            pltpu.VMEM((cb, bs, bs), f32),
            pltpu.VMEM((cb + 1, bs, bs), bf),
            pltpu.VMEM((n, rb, tile, bs), bf),
            pltpu.VMEM((n - 1, rb, tile, bs), bf),
            pltpu.VMEM((n, rb, tile, bs), bf),
            pltpu.VMEM((n - 1, rb, tile, bs), bf),
            pltpu.VMEM((rb, tile, bs), bf),
            pltpu.VMEM((HIGH, CORES, rb, n, tile, bs), bf),
            pltpu.VMEM((rb, tile, bs), bf),
            pltpu.VMEM((cb, bs), jnp.int32),
            pltpu.SMEM((cb, bs), jnp.int32),
            pltpu.VMEM((rb, bs, bs), f32),
            dma((rb,)), dma(()), dma(()),
            dma(()), dma(()),
            dma(()), dma(()),
            dma(()), dma(()),
            dma((batches,)), dma((batches,)),
            dma((batches,)), dma((batches,)),
            dma((batches, 2)), dma((batches,)),
            dma((batches,)), dma((batches,)),
            dma((batches, HIGH)), dma((batches, HIGH)),
            dma((batches,)), dma((batches,)),
            dma((batches,)),
        ],
        compiler_params=pltpu.CompilerParams(
            collective_id=0, has_side_effects=True, vmem_limit_bytes=56 * 2**20
        ),
    )(
        blocks, slot_cols, slot_cols, counts.T, demand.reshape(cb, bs, bs), value_added.reshape(cb, bs)
    )
    return result.reshape(rb * bs, bs)


def solution(mesh):
    rows, n = mesh.shape["row"], mesh.shape["col"]
    return jax.shard_map(
        functools.partial(body, rows, n),
        mesh=mesh,
        in_specs=(
            P("row", "col", None, None),
            P("row", "col"),
            P("row", "col"),
            P("col", None),
            P("col"),
        ),
        out_specs=P("row", None),
        check_vma=False,
    )
```

```python
import functools

import jax
import jax.numpy as jnp
from jax import lax
from jax.experimental import pallas as pl
from jax.experimental.pallas import tpu as pltpu
from jax.sharding import PartitionSpec as P

MESH = pl.DeviceIdType.MESH
HIGH = 2
CORES = 2
WIDE = 4


def kernel(
    rows, n, groups,
    blocks, cols_s, cols_v, counts_s, demand_hbm, added, out,
    zbuf, demand, sums, tsend, trecv, bsend, brecv, tall, spread, scaled,
    part, rs_recv, part2, rs_recv2, first, source, piece, places, place_s, so_far,
    zsem, dsem, place_sem, t_send, t_recv, b_send, b_recv, a_send, a_recv,
    rs_send, rs_sem, rs_send2, rs_sem2, p_send, p_recv,
    y_send, y_recv, c_send, c_recv, o_send, o_recv, o_local,
):
    zs = rows // (HIGH * CORES)
    rb, slots, bs = zbuf.shape[0], zbuf.shape[1], zbuf.shape[2]
    cb = demand.shape[0]
    per_core = cb // CORES
    chips = rows // CORES
    targets = n // HIGH
    tile = bs // n
    batches = len(groups)
    step = 2
    row, col = lax.axis_index("row"), lax.axis_index("col")
    core = row % CORES
    z = (row // CORES) % zs
    high = row // (CORES * zs)

    def rid(h, zz, k):
        return (h * zs + zz) * CORES + k

    def wrap(i, count):
        return jnp.where(i >= count, i - count, i)

    def remote(src, dst, send, recv, to):
        return pltpu.make_async_remote_copy(
            src_ref=src, dst_ref=dst, send_sem=send, recv_sem=recv, device_id=to, device_id_type=MESH
        )

    def span(g):
        return pl.ds(groups[g][0], groups[g][1] - groups[g][0])

    def each(count, fn, first=0):
        def body(i, c):
            fn(i)
            return c

        lax.fori_loop(first, count, body, 0)

    def settle(ref, sem):
        pltpu.make_async_copy(ref, ref, sem).wait()

    def load(b):
        return pltpu.make_async_copy(blocks.at[b], zbuf.at[b], zsem.at[b])

    each(rb, lambda b: load(b).start())
    load_demand = pltpu.make_async_copy(demand_hbm, demand, dsem)
    load_demand.start()

    buyer = row // (rows // n)
    side = z % HIGH
    giver = rid(col // targets, (col % targets) * HIGH + high, core)
    is_self = (side == high) & (buyer == col)
    here = row // CORES

    def chip(d):
        return wrap(here + d, chips) * CORES + core

    barrier = pltpu.get_barrier_semaphore()

    def greet(to):
        pl.semaphore_signal(barrier, inc=1, device_id=to, device_id_type=MESH)

    each(chips, lambda d: greet((chip(d), col)), 1)
    greet((rid(high, z, 1 - core), col))
    each(n, lambda d: greet((row, wrap(col + d, n))), 1)

    def greet_giver(c):
        @pl.when(jnp.logical_not((giver == row) & (c == col)))
        def _():
            greet((giver, c))

    each(n, greet_giver)

    group = lax.broadcasted_iota(jnp.int32, (cb, slots), 0)
    slot = lax.broadcasted_iota(jnp.int32, (cb, slots), 1)

    lane = lax.broadcasted_iota(jnp.int32, (cb, bs), 1)

    def add_row(b, carry):
        total, place = carry
        load(b).wait()
        for s in range(slots):
            sums[pl.ds(s, 1), :] = jnp.sum(zbuf[b, s].astype(jnp.float32), axis=0, keepdims=True)
        hit = (group == cols_v[pl.ds(b, 1), :]) & (slot < counts_s[0, b])
        found = jnp.sum(jnp.where(hit, slot + 1, 0), axis=1, keepdims=True)
        place = jnp.where(lane == b, found, place)
        total = total + jnp.dot(
            hit.astype(jnp.float32), sums[...], precision=lax.Precision.HIGHEST,
            preferred_element_type=jnp.float32,
        )
        return total, place

    total, place = lax.fori_loop(
        0, rb, add_row, (jnp.zeros((cb, bs), jnp.float32), jnp.zeros((cb, bs), jnp.int32))
    )
    places[...] = place
    move = pltpu.make_async_copy(places, place_s, place_sem)
    move.start()
    for k in range(CORES):
        tsend[k] = total[k * per_core : (k + 1) * per_core]
    load_demand.wait()
    move.wait()

    pl.semaphore_wait(barrier, (chips - 1) + 1 + (n - 1) + zs - jnp.where(is_self, 1, 0))

    twin = (rid(high, z, 1 - core), col)
    swap = remote(tsend.at[1 - core], trecv, t_send, t_recv, twin)
    swap.start()
    swap.wait()
    mine = tsend[core] + trecv[...]
    bsend[...] = jnp.concatenate(
        [mine, jnp.zeros((bsend.shape[0] - per_core, bs), jnp.float32)], axis=0
    ).astype(jnp.bfloat16)

    def b_copy(d):
        return remote(bsend, brecv.at[d - 1], b_send, b_recv, (chip(d), col))

    each(chips, lambda d: b_copy(d).start(), 1)
    settle(brecv, b_recv)
    for d in range(chips - 1):
        mine = mine + brecv[d].astype(jnp.float32)[:per_core]
    tall[core] = mine
    give_half = remote(tall.at[core], tall.at[core], a_send, a_recv, twin)
    give_half.start()
    settle(brecv, b_send)
    give_half.wait_send()
    remote(tall.at[1 - core], tall.at[1 - core], a_send, a_recv, twin).wait_recv()

    totals = jnp.concatenate([tall[k] for k in range(CORES)], axis=0) + added[...]
    inverse = 1.0 / totals
    padded = jnp.concatenate([inverse, jnp.zeros((bs - cb, bs), jnp.float32)], axis=0)
    turned = padded.T
    for j in range(cb):
        wide = jnp.broadcast_to(turned[:, j : j + 1], (bs, bs))
        spread[j] = wide
        scaled[j] = (demand[j].astype(jnp.float32) * wide).astype(jnp.bfloat16)
    scaled[cb] = jnp.zeros((bs, bs), jnp.bfloat16)

    def exchange(into, recv, send_sem, recv_sem, finish, after):
        def rs_copy(g, d):
            to = wrap(col + d, n)
            at = span(g)
            return remote(into.at[to, at], recv.at[d - 1, at], send_sem.at[g], recv_sem.at[g], (row, to))

        def start(g):
            each(n, lambda d: rs_copy(g, d).start(), 1)

        def reduce(g):
            settle(recv.at[:, span(g)], recv_sem.at[g])
            for b in range(*groups[g]):
                acc = into[col, b].astype(jnp.float32)
                for d in range(n - 1):
                    acc = acc + recv[d, b].astype(jnp.float32)
                finish(b, acc)
            after(g)

        def sent():
            for g in range(batches):
                settle(recv.at[:, span(g)], send_sem.at[g])

        return start, reduce, sent

    def product(acc, b, pairs):
        left = jnp.concatenate([zbuf[b, t] for t, _ in pairs], axis=1)
        right = jnp.concatenate([scaled[a] for _, a in pairs], axis=0)
        return acc + jnp.dot(left, right, preferred_element_type=jnp.float32)

    def compute(i):
        accs = [jnp.zeros((bs, bs), jnp.float32) for _ in range(step)]
        wide = WIDE if slots % WIDE == 0 else 2
        for s in range(0, slots, wide):
            for k in range(step):
                b = i * step + k
                live = counts_s[0, b]
                pairs = [(t, jnp.where(t < live, cols_s[b, t], cb)) for t in range(s, s + wide)]
                accs[k] = product(accs[k], b, pairs)
        for k in range(step):
            part[:, i * step + k] = accs[k].astype(jnp.bfloat16).reshape(n, tile, bs)

    def keep(b, acc):
        first[b] = acc.astype(jnp.bfloat16)

    def p_copy(i, d):
        src = first.at[span(i)]
        dst = source.at[side, core, span(i), col]
        to = (rid(side, wrap(z + d, zs), core), buyer)
        return src, dst, remote(src, dst, p_send.at[i, jnp.minimum(d, 1)], p_recv.at[i], to)

    def spread_out(i):
        src, dst, far = p_copy(i, 0)

        @pl.when(is_self)
        def _():
            pltpu.make_async_copy(src, dst, p_recv.at[i]).start()

        @pl.when(jnp.logical_not(is_self))
        def _():
            far.start()

        each(zs, lambda d: p_copy(i, d)[2].start(), 1)

    def spread_sent(i):
        @pl.when(jnp.logical_not(is_self))
        def _():
            p_copy(i, 0)[2].wait_send()

        settle(source.at[high, core, span(i), pl.ds(0, zs - 1)], p_send.at[i, 1])

    start_one, reduce_one, sent_one = exchange(part, rs_recv, rs_send, rs_sem, keep, spread_out)
    for g in range(batches):
        each(groups[g][1] // step, compute, groups[g][0] // step)
        start_one(g)
    for g in range(batches):
        reduce_one(g)

    def y_copy(i):
        at = source.at[high, core, span(i)]
        return remote(at, at, y_send.at[i], y_recv.at[i], (rid(1 - high, z, core), col))

    def y_arrived(i):
        at = source.at[1 - high, core, span(i)]
        remote(at, at, y_send.at[i], y_recv.at[i], (row, col)).wait_recv()

    def c_copy(i, h):
        at = source.at[h, core, span(i)]
        return remote(at, at, c_send.at[i, h], c_recv.at[i, h], twin)

    def c_arrived(i, h):
        at = source.at[h, 1 - core, span(i)]
        remote(at, at, c_send.at[i, h], c_recv.at[i, h], twin).wait_recv()

    def pass_on(i):
        settle(source.at[high, core, span(i)], p_recv.at[i])
        y_copy(i).start()
        c_copy(i, high).start()

    def pass_back(i):
        y_arrived(i)
        c_copy(i, 1 - high).start()

    def result(b, acc):
        piece[b] = (first[b].astype(jnp.float32) + acc).astype(jnp.bfloat16)

    def o_copy(i, d):
        at = span(i)
        return remote(
            piece.at[at], out.at[at, col], o_send.at[i], o_recv.at[i], (row, wrap(col + d, n))
        )

    def o_own(i):
        at = span(i)
        return pltpu.make_async_copy(piece.at[at], out.at[at, col], o_local.at[i])

    def give(i):
        each(n, lambda d: o_copy(i, d).start(), 1)
        o_own(i).start()

    start_two, reduce_two, sent_two = exchange(part2, rs_recv2, rs_send2, rs_sem2, result, give)

    def advance(g):
        lo, hi = groups[g]
        for h in range(HIGH):
            c_arrived(g, h)
        cols_of = [q * rb + b for q in range(HIGH * CORES) for b in range(lo, hi)]
        for j in cols_of:
            q, b = j // rb, j % rb
            value = source[q // CORES, q % CORES, b].reshape(bs, bs).astype(jnp.float32)
            scaled[j] = (value * spread[j]).astype(jnp.bfloat16)

        def rows_of(i):
            accs = [so_far[i * step + k] if g else jnp.zeros((bs, bs), jnp.float32) for k in range(step)]
            for s in range(0, len(cols_of), WIDE):
                for k in range(step):
                    b = i * step + k
                    pairs = []
                    for j in cols_of[s : s + WIDE]:
                        at = place_s[j, b]
                        pairs.append((jnp.maximum(at - 1, 0), jnp.where(at > 0, j, cb)))
                    accs[k] = product(accs[k], b, pairs)
            for k in range(step):
                if g < batches - 1:
                    so_far[i * step + k] = accs[k]
                else:
                    part2[:, i * step + k] = accs[k].astype(jnp.bfloat16).reshape(n, tile, bs)

        if g < batches - 1:
            each(rb // step, rows_of)
        else:
            for k in range(batches):
                each(groups[k][1] // step, rows_of, groups[k][0] // step)
                start_two(k)

    for g in range(batches):
        pass_on(g)
        if g >= 2:
            advance(g - 2)
        if g >= 1:
            pass_back(g - 1)
    pass_back(batches - 1)
    for g in range(max(batches - 2, 0), batches):
        advance(g)
    for g in range(batches):
        reduce_two(g)

    for g in range(batches):
        spread_sent(g)

    def passed(i):
        y_copy(i).wait_send()
        for h in range(HIGH):
            c_copy(i, h).wait_send()

    for g in range(batches):
        passed(g)
    sent_one()
    sent_two()

    for g in range(batches):
        like = rs_recv2.at[:, span(g)]
        settle(like, o_recv.at[g])
        settle(like, o_send.at[g])
        o_own(g).wait()


def body(rows, n, blocks, slot_cols, counts, demand, value_added):
    rb, slots, bs = blocks.shape[0], blocks.shape[1], blocks.shape[2]
    cb = demand.shape[0] // bs
    zs = rows // (HIGH * CORES)
    tile = bs // n
    cuts = sorted({0, rb * 2 // 5 // 2 * 2, rb * 4 // 5 // 2 * 2, rb})
    groups = tuple(zip(cuts, cuts[1:]))
    batches = len(groups)
    per_core, chips = cb // CORES, rows // CORES
    bf, f32, dma = jnp.bfloat16, jnp.float32, pltpu.SemaphoreType.DMA
    vmem, smem, hbm = (
        pl.BlockSpec(memory_space=pltpu.VMEM), pl.BlockSpec(memory_space=pltpu.SMEM), pl.BlockSpec(memory_space=pl.ANY)
    )
    result = pl.pallas_call(
        functools.partial(kernel, rows, n, groups),
        out_shape=jax.ShapeDtypeStruct((rb, n, tile, bs), bf),
        in_specs=[hbm, smem, vmem, smem, hbm, vmem],
        out_specs=hbm,
        scratch_shapes=[
            pltpu.VMEM((rb, slots, bs, bs), bf),
            pltpu.VMEM((cb, bs, bs), bf),
            pltpu.VMEM((slots, bs), f32),
            pltpu.VMEM((CORES, per_core, bs), f32),
            pltpu.VMEM((per_core, bs), f32),
            pltpu.VMEM((-(-per_core // 16) * 16, bs), bf),
            pltpu.VMEM((chips - 1, -(-per_core // 16) * 16, bs), bf),
            pltpu.VMEM((CORES, per_core, bs), f32),
            pltpu.VMEM((cb, bs, bs), f32),
            pltpu.VMEM((cb + 1, bs, bs), bf),
            pltpu.VMEM((n, rb, tile, bs), bf),
            pltpu.VMEM((n - 1, rb, tile, bs), bf),
            pltpu.VMEM((n, rb, tile, bs), bf),
            pltpu.VMEM((n - 1, rb, tile, bs), bf),
            pltpu.VMEM((rb, tile, bs), bf),
            pltpu.VMEM((HIGH, CORES, rb, n, tile, bs), bf),
            pltpu.VMEM((rb, tile, bs), bf),
            pltpu.VMEM((cb, bs), jnp.int32),
            pltpu.SMEM((cb, bs), jnp.int32),
            pltpu.VMEM((rb, bs, bs), f32),
            dma((rb,)), dma(()), dma(()),
            dma(()), dma(()),
            dma(()), dma(()),
            dma(()), dma(()),
            dma((batches,)), dma((batches,)),
            dma((batches,)), dma((batches,)),
            dma((batches, 2)), dma((batches,)),
            dma((batches,)), dma((batches,)),
            dma((batches, HIGH)), dma((batches, HIGH)),
            dma((batches,)), dma((batches,)),
            dma((batches,)),
        ],
        compiler_params=pltpu.CompilerParams(
            collective_id=0, has_side_effects=True, vmem_limit_bytes=56 * 2**20
        ),
    )(
        blocks, slot_cols, slot_cols, counts.T, demand.reshape(cb, bs, bs), value_added.reshape(cb, bs)
    )
    return result.reshape(rb * bs, bs)


def solution(mesh):
    rows, n = mesh.shape["row"], mesh.shape["col"]
    return jax.shard_map(
        functools.partial(body, rows, n),
        mesh=mesh,
        in_specs=(
            P("row", "col", None, None),
            P("row", "col"),
            P("row", "col"),
            P("col", None),
            P("col"),
        ),
        out_specs=P("row", None),
        check_vma=False,
    )
```
